32 devices in a mesh: island: 8 (over z, x), fsdp: 4 (over y, core).
Axes of the slice: x: 2, y: 2, z: 4, core: 2. Of those that a mesh axis runs over, the one named last changes fastest.
Arguments:
- pseudo_grad: bfloat16 [8, 8192, 512], P('island', 'fsdp'), may hold values from -40 to 40
- error_buf: bfloat16 [8, 8192, 512], P('island', 'fsdp'), may hold values from -2 to 2
- params: bfloat16 [8192, 512], P('fsdp'), may hold values from -6 to 6
- momentum: float32 [8, 12288], P('island', 'fsdp'), may hold values from -4 to 4
- sel_blocks: int32 [8, 512], P('island', 'fsdp'), may hold values from 0 to 255, as said below
- coef_index: int32 [1024, 64], P('fsdp'), may hold values from 0 to 4095, as said below
- owner_map: int32 [1024], P('fsdp'), may hold values from 0 to 7, as said below
Outputs:
- new_params: bfloat16 [8192, 512], P('fsdp')
- new_error: bfloat16 [8, 8192, 512], P('island', 'fsdp')
- new_momentum: float32 [8, 12288], P('island', 'fsdp')
The draws below stay inside these ranges and needn't reach their ends.
Inputs may be any that keep to these rules, and one draw needn't show every extreme that they name: `sel_blocks`: each island's 128 entries for one shard are distinct blocks of that shard. `coef_index`: each row holds 64 distinct positions. `owner_map`: within each shard of 256 blocks an island owns at most 48 blocks, and some island owns exactly 48.
All inputs are finite; a program needn't handle non-finite values.
Results may differ from the reference program's by a relative error of at most 0.0032.
Values may be sent and summed in bfloat16 or wider, within the bound.
A program may use at most 64 MiB of HBM per device.

```python
import jax
import jax.numpy as jnp
from jax import lax

D = 8192
KV_HEADS = 4
HEAD_DIM = 128
COEFS = 64
KVW = 512
BLK_DEV = 256
SEL = 128
OWN_CAP = 48
N_ISLAND = 8
N_FSDP = 4


def rising_factor(shard_pos):
    return 3.0 ** (shard_pos.astype(jnp.float32) / max(N_FSDP - 1, 1))


def draw_pseudo_grad(key, part):
    columns = KV_HEADS * HEAD_DIM
    subkeys = jax.random.split(jax.random.fold_in(key, 11), 5)
    row_scale = 10.0 ** jax.random.uniform(subkeys[0], (N_ISLAND, D, 1))
    col_scale = 10.0 ** jax.random.uniform(subkeys[1], (N_ISLAND, 1, columns))
    shard_pos = jnp.arange(D) // (D // N_FSDP)
    rising = rising_factor(shard_pos)[None, :, None]
    values_base = jax.random.normal(subkeys[4], (N_ISLAND, D, columns))
    return jnp.clip(values_base * row_scale * col_scale * rising / 6.0, -40.0, 40.0).astype(jnp.bfloat16)


def draw_momentum(key, part):
    per_shard = OWN_CAP * COEFS
    subkeys = jax.random.split(jax.random.fold_in(key, 23), 2)
    shard_pos = jnp.arange(N_FSDP * per_shard) // per_shard
    rising = rising_factor(shard_pos)[None, :]
    values_base = jax.random.normal(subkeys[1], (N_ISLAND, N_FSDP * per_shard))
    return jnp.clip(0.5 * values_base * rising, -4.0, 4.0)


def draw_sel_blocks(key, part):
    held_keys = jax.random.split(jax.random.fold_in(key, 53), 2)
    held_shard = jax.random.randint(held_keys[0], (), 0, N_FSDP).astype(jnp.int32)
    held_block = jax.random.randint(held_keys[1], (), 0, BLK_DEV).astype(jnp.int32)
    subkeys = jax.random.split(jax.random.fold_in(key, 31), N_ISLAND * N_FSDP)
    shard_pos = (jnp.arange(N_ISLAND * N_FSDP) % N_FSDP).astype(jnp.int32)

    def one_list(single, shard_here):
        full_list = jax.random.permutation(single, BLK_DEV)[:SEL].astype(jnp.int32)
        short_list = jax.random.permutation(single, BLK_DEV - 1)[:SEL].astype(jnp.int32)
        short_list = short_list + (short_list >= held_block).astype(jnp.int32)
        return jnp.where(shard_here == held_shard, short_list, full_list)
    picks = jax.vmap(one_list)(subkeys, shard_pos)
    return picks.reshape(N_ISLAND, N_FSDP * SEL).astype(jnp.int32)


def draw_coef_index(key, part):
    subkeys = jax.random.split(jax.random.fold_in(key, 37), N_FSDP * BLK_DEV)
    picks = jax.vmap(lambda single: jax.random.permutation(single, 4096)[:COEFS])(subkeys)
    return picks.astype(jnp.int32)


def owners_of_shard(single):
    first_key, second_key = jax.random.split(single)
    slot_total = N_ISLAND * OWN_CAP
    shuffled = jax.random.permutation(first_key, slot_total)
    leading = shuffled[0] // OWN_CAP
    slot_ids = jnp.arange(slot_total)
    position = jnp.argsort(shuffled)
    scores = jnp.where(slot_ids // OWN_CAP == leading, slot_ids - slot_total, position)
    ordering = jnp.argsort(scores)
    owners = ordering[:BLK_DEV] // OWN_CAP
    mixing = jax.random.permutation(second_key, BLK_DEV)
    return owners[mixing]


def draw_owner_map(key, part):
    subkeys = jax.random.split(jax.random.fold_in(key, 41), N_FSDP)
    return jax.vmap(owners_of_shard)(subkeys).reshape(N_FSDP * BLK_DEV).astype(jnp.int32)


def levels(key, extent, pieces, smallest, high):
    factor_of, own = 1.0, jax.random.fold_in(key, 6)
    for dim, shards_of in pieces:
        heights = jnp.exp(jax.random.uniform(jax.random.fold_in(own, dim), (shards_of,), jnp.float32, smallest / len(pieces), high / len(pieces)))
        factor_of = factor_of * jnp.repeat(heights, extent[dim] // shards_of).reshape([-1 if axis == dim else 1 for axis in range(len(extent))])
    return factor_of


def noise(stream_key, extent, scale, bound, cuts=(), kind=jnp.bfloat16):
    entries = scale * jax.random.normal(stream_key, extent, jnp.float32)
    if cuts:
        entries = entries * levels(stream_key, extent, cuts, -0.22, 0.18)
    return jnp.clip(entries, -bound, bound).astype(kind)


def setup_inputs(seed: int = 0) -> dict:
    key_of = jax.random.split(jax.random.key(seed), 8)
    return {
        "pseudo_grad": draw_pseudo_grad(jax.random.fold_in(key_of[7], 71), 0),
        "error_buf": noise(key_of[1], (N_ISLAND, D, KVW), 0.3, 2.0, ((0, 8), (1, 4))),
        "params": noise(key_of[2], (D, KVW), 1.0, 6.0, ((0, 4),)),
        "momentum": draw_momentum(jax.random.fold_in(key_of[7], 71), 0),
        "sel_blocks": draw_sel_blocks(jax.random.fold_in(key_of[7], 71), 0),
        "coef_index": draw_coef_index(jax.random.fold_in(key_of[7], 71), 0),
        "owner_map": draw_owner_map(jax.random.fold_in(key_of[7], 71), 0),
    }


BETA_FACTOR = 0.9
OUTER_RATE = 0.5
EPSILON = 1e-06
precise_mode = lax.Precision.HIGHEST

def cosine_table():
    freqs = jnp.arange(64, dtype=jnp.float32)[:, None]
    points = jnp.arange(64, dtype=jnp.float32)[None, :]
    scaling = jnp.where(freqs == 0.0, jnp.sqrt(1.0 / 64.0), jnp.sqrt(2.0 / 64.0))
    return scaling * jnp.cos(jnp.pi * (2.0 * points + 1.0) * freqs / 128.0)

def to_blocks(field):
    row_blocks = field.shape[0] // 64
    col_blocks = field.shape[1] // 64
    return field.reshape(row_blocks, 64, col_blocks, 64).transpose(0, 2, 1, 3).reshape(row_blocks * col_blocks, 64, 64)

def from_blocks(blocks, row_total, col_total):
    row_blocks = row_total // 64
    col_blocks = col_total // 64
    return blocks.reshape(row_blocks, col_blocks, 64, 64).transpose(0, 2, 1, 3).reshape(row_total, col_total)

def forward_blocks(cosine, blocks):
    return jnp.einsum('ij,bjk,lk->bil', cosine, blocks, cosine, precision=precise_mode)

def inverse_blocks(cosine, blocks):
    return jnp.einsum('ji,bjk,kl->bil', cosine, blocks, cosine, precision=precise_mode)

def scatter_coefs(values, positions):
    amount = values.shape[0]
    return jnp.zeros((amount, 4096), jnp.float32).at[jnp.arange(amount)[:, None], positions].set(values)

def reference(pseudo_grad, error_buf, params, momentum, sel_blocks, coef_index, owner_map):
    cosine = cosine_table()
    n_blocks = coef_index.shape[0]
    shard_blocks = n_blocks // N_FSDP
    shard_picks = sel_blocks.shape[1] // N_FSDP
    coef_count = coef_index.shape[1]
    block_ids = jnp.arange(n_blocks, dtype=jnp.int32)
    shard_of = block_ids // shard_blocks
    offsets = (jnp.arange(N_FSDP, dtype=jnp.int32) * shard_blocks)[:, None]

    def island_step(inputs):
        grad_part, error_part, chosen = inputs
        summed = grad_part.astype(jnp.float32) + error_part.astype(jnp.float32)
        blocks = to_blocks(summed)
        spectra = forward_blocks(cosine, blocks).reshape(n_blocks, 4096)
        picked = jnp.take_along_axis(spectra, coef_index, axis=1)
        global_ids = (chosen.reshape(N_FSDP, shard_picks) + offsets).reshape(-1)
        chosen_mask = jnp.zeros((n_blocks,), jnp.float32).at[global_ids].set(1.0)
        outgoing = picked * chosen_mask[:, None]
        rebuilt = inverse_blocks(cosine, scatter_coefs(outgoing, coef_index).reshape(n_blocks, 64, 64))
        fresh_error = from_blocks(blocks - rebuilt, summed.shape[0], summed.shape[1]).astype(jnp.bfloat16)
        return (fresh_error, outgoing, chosen_mask)
    new_error, outgoing_all, masks_all = lax.map(island_step, (pseudo_grad, error_buf, sel_blocks))
    totals = lax.optimization_barrier(jnp.sum(outgoing_all, axis=0))
    counts = lax.optimization_barrier(jnp.sum(masks_all, axis=0))
    average = totals / jnp.maximum(counts, 1.0)[:, None]
    earlier = (owner_map[None, :] == owner_map[:, None]) & (shard_of[None, :] == shard_of[:, None]) & (block_ids[None, :] < block_ids[:, None])
    slot_of = lax.optimization_barrier(jnp.sum(earlier.astype(jnp.int32), axis=1))
    capacity = momentum.shape[1] // (N_FSDP * coef_count)
    grouped = momentum.reshape(N_ISLAND, N_FSDP, capacity, coef_count)
    previous = grouped[owner_map, shard_of, slot_of]
    refreshed = BETA_FACTOR * previous + average
    new_grouped = (BETA_FACTOR * grouped).at[owner_map, shard_of, slot_of].set(refreshed)
    update_coef = average + BETA_FACTOR * refreshed
    update = inverse_blocks(cosine, scatter_coefs(update_coef, coef_index).reshape(n_blocks, 64, 64)).astype(jnp.bfloat16)
    update = lax.optimization_barrier(update).astype(jnp.float32)
    total_square = jnp.sum(update * update)
    scale_root = jnp.sqrt(total_square / (D * KVW) + EPSILON)
    shifted = from_blocks(update, D, KVW)
    new_params = (params.astype(jnp.float32) - OUTER_RATE * shifted / scale_root).astype(jnp.bfloat16)
    return (new_params, new_error, new_grouped.reshape(N_ISLAND, N_FSDP * capacity * coef_count))
```

```python
import functools

import numpy as np

import jax
import jax.numpy as jnp
from jax import lax
from jax.experimental import pallas as pl
from jax.experimental.pallas import tpu as pltpu
from jax.sharding import PartitionSpec as P

BETA_FACTOR = 0.9
OUTER_RATE = 0.5
EPSILON = 1e-06
precise_mode = lax.Precision.HIGHEST


def cosine_table():
    freqs = jnp.arange(64, dtype=jnp.float32)[:, None]
    points = jnp.arange(64, dtype=jnp.float32)[None, :]
    scaling = jnp.where(freqs == 0.0, jnp.sqrt(1.0 / 64.0), jnp.sqrt(2.0 / 64.0))
    return scaling * jnp.cos(jnp.pi * (2.0 * points + 1.0) * freqs / 128.0)


def to_blocks(field):
    row_blocks = field.shape[0] // 64
    col_blocks = field.shape[1] // 64
    return (
        field.reshape(row_blocks, 64, col_blocks, 64)
        .transpose(0, 2, 1, 3)
        .reshape(row_blocks * col_blocks, 64, 64)
    )


def from_blocks(blocks, row_total, col_total):
    row_blocks = row_total // 64
    col_blocks = col_total // 64
    return (
        blocks.reshape(row_blocks, col_blocks, 64, 64)
        .transpose(0, 2, 1, 3)
        .reshape(row_total, col_total)
    )


def forward_blocks(cosine, blocks):
    return jnp.einsum("ij,bjk,lk->bil", cosine, blocks, cosine, precision=precise_mode)


def inverse_blocks(cosine, blocks):
    return jnp.einsum("ji,bjk,kl->bil", cosine, blocks, cosine, precision=precise_mode)


def scatter_coefs(values, positions):
    amount = values.shape[0]
    return (
        jnp.zeros((amount, 4096), jnp.float32)
        .at[jnp.arange(amount)[:, None], positions]
        .set(values)
    )


def plain_on_device(pseudo_grad, error_buf, params, momentum, sel_blocks, coef_index, owner_map):
    cosine = cosine_table()
    islands = lax.axis_size("island")
    my_island = lax.axis_index("island")
    shard_rows = params.shape[0]
    columns = params.shape[1]
    n_blocks = coef_index.shape[0]
    coef_total = coef_index.shape[1]
    capacity = momentum.shape[1] // coef_total
    summed = pseudo_grad[0].astype(jnp.float32) + error_buf[0].astype(jnp.float32)
    blocks = to_blocks(summed)
    spectra = forward_blocks(cosine, blocks).reshape(n_blocks, 4096)
    picked = jnp.take_along_axis(spectra, coef_index, axis=1)
    chosen = sel_blocks[0]
    block_ids = jnp.arange(n_blocks, dtype=jnp.int32)
    chosen_mask = jnp.any(chosen[:, None] == block_ids[None, :], axis=0).astype(jnp.float32)
    outgoing = picked * chosen_mask[:, None]
    rebuilt = inverse_blocks(cosine, scatter_coefs(outgoing, coef_index).reshape(n_blocks, 64, 64))
    new_error = from_blocks(blocks - rebuilt, shard_rows, columns).astype(jnp.bfloat16)[None]
    earlier = (owner_map[None, :] == owner_map[:, None]) & (block_ids[None, :] < block_ids[:, None])
    slot_of = jnp.sum(earlier.astype(jnp.int32), axis=1)
    target = owner_map * capacity + slot_of
    own_slots = my_island * capacity + jnp.arange(capacity, dtype=jnp.int32)
    owned_mask = target[None, :] == own_slots[:, None]
    owned_ids = jnp.sum(jnp.where(owned_mask, block_ids[None, :], 0), axis=1)
    owned_live = jnp.any(owned_mask, axis=1)
    owned_pattern = jnp.sum(jnp.where(owned_mask[:, :, None], coef_index[None, :, :], 0), axis=1)
    listed = outgoing[chosen]
    piece_values = lax.all_gather(listed, "island", axis=0, tiled=True)
    piece_ids = lax.all_gather(chosen, "island", axis=0, tiled=True)
    matches = ((piece_ids[None, :] == owned_ids[:, None]) & owned_live[:, None]).astype(jnp.float32)
    totals = jnp.dot(matches, piece_values, precision=precise_mode)
    counts = jnp.sum(matches, axis=1)
    average = totals / jnp.maximum(counts, 1.0)[:, None]
    previous = momentum[0].reshape(capacity, coef_total)
    refreshed = BETA_FACTOR * previous + average
    update_coef = average + BETA_FACTOR * refreshed
    new_momentum = refreshed.reshape(1, capacity * coef_total)
    owner_dense = inverse_blocks(
        cosine, scatter_coefs(update_coef, owned_pattern).reshape(capacity, 64, 64)
    )
    owner_dense = owner_dense.reshape(capacity, 4096).astype(jnp.bfloat16)
    gathered_dense = lax.all_gather(owner_dense, "island", axis=0, tiled=True)
    selector = (target[:, None] == jnp.arange(islands * capacity, dtype=jnp.int32)[None, :]).astype(
        jnp.bfloat16
    )
    received = jnp.dot(selector, gathered_dense, preferred_element_type=jnp.float32)
    local_square = jnp.sum(received * received)
    total_square = lax.psum(local_square, "fsdp")
    scale_root = jnp.sqrt(total_square / (shard_rows * lax.axis_size("fsdp") * columns) + EPSILON)
    shifted = from_blocks(received.reshape(n_blocks, 64, 64), shard_rows, columns)
    new_params = (params.astype(jnp.float32) - OUTER_RATE * shifted / scale_root).astype(
        jnp.bfloat16
    )
    return (new_params, new_error, new_momentum)


MESH = pl.DeviceIdType.MESH
TILE = 256
F32 = jnp.float32
BF16 = jnp.bfloat16


def cosine_parts():
    freqs = np.arange(64)[:, None]
    points = np.arange(64)[None, :]
    scaling = np.where(freqs == 0, np.sqrt(1.0 / 64.0), np.sqrt(2.0 / 64.0))
    cosine = scaling * np.cos(np.pi * (2.0 * points + 1.0) * freqs / 128.0)
    diagonal = np.kron(np.eye(4), cosine).astype(np.float32)
    parts = []
    for table in (diagonal, diagonal.T):
        high = table.astype(BF16)
        parts += [high, (table - high.astype(np.float32)).astype(BF16)]
    return np.stack(parts)


def iota(shape, dim):
    return lax.broadcasted_iota(jnp.int32, shape, dim)


def split(value):
    high = value.astype(BF16)
    return high, (value - high.astype(F32)).astype(BF16)


def dot(a, b):
    return jnp.dot(a, b, preferred_element_type=F32)


def exact_dot(a, b, dims):
    return lax.dot_general(
        a, b, (dims, ((), ())), precision=precise_mode, preferred_element_type=F32
    )


def times_table(parts, table):
    rows = parts[0].shape[0]
    both = dot(jnp.concatenate(parts, axis=0), table[0])
    return both[:rows] + both[rows:] + dot(parts[0], table[1])


def table_times(table, parts):
    return dot(table[0], parts[0]) + dot(table[0], parts[1]) + dot(table[1], parts[0])


def unit_masks(positions):
    rows = lax.shift_right_logical(positions, 6)
    cols = (positions & 63) + (iota((1, TILE), 1) & -64)
    row_mask = iota((64, TILE), 0) == rows
    col_mask = jnp.where(iota((TILE, TILE), 0) == cols, 1.0, 0.0).astype(BF16)
    return row_mask, col_mask


def gather_unit(spectrum, positions):
    row_mask, col_mask = unit_masks(positions)
    both = dot(jnp.concatenate(split(spectrum), axis=0), col_mask)
    return jnp.sum(jnp.where(row_mask, both[:64] + both[64:], 0.0), axis=0, keepdims=True)


def scatter_unit(values, positions):
    row_mask, col_mask = unit_masks(positions)
    high, low = split(jnp.where(row_mask, values, 0.0))
    both = lax.dot_general(
        jnp.concatenate([high, low], axis=0),
        col_mask,
        (((1,), (1,)), ((), ())),
        preferred_element_type=F32,
    ).astype(BF16)
    return both[:64], both[64:]


def decode_tile(values, positions, half, forward, backward):
    highs, lows = [], []
    for strip in range(4):
        unit = 2 * strip + half
        high, low = scatter_unit(values[unit : unit + 1], positions[unit : unit + 1])
        highs.append(high)
        lows.append(low)
    parts = (jnp.concatenate(highs, axis=0), jnp.concatenate(lows, axis=0))
    return table_times(backward, split(times_table(parts, forward)))


def kernel(
    n,
    m,
    elements,
    grad_ref,
    err_ref,
    params_ref,
    mom_ref,
    sel_row_ref,
    sel_col_ref,
    index_ref,
    owner_row_ref,
    owner_col_ref,
    table_ref,
    new_params_ref,
    new_err_ref,
    new_mom_ref,
    early,
    early_in,
    sent,
    sent_in,
    coefs,
    update,
    squares,
    squares_in,
    early_send,
    early_recv,
    sent_send,
    sent_recv,
    coefs_send,
    coefs_recv,
    squares_send,
    squares_recv,
):
    me = lax.axis_index("island")
    shard = lax.axis_index("fsdp")
    units, width = index_ref.shape
    slots, kept = mom_ref.shape
    n_blocks = owner_col_ref.shape[0]

    def island_peer(d):
        return lax.rem(me + d, n)

    def island_source(d):
        return lax.rem(me - d + n, n)

    barrier = pltpu.get_barrier_semaphore()
    for d in range(1, n):
        pl.semaphore_signal(barrier, inc=1, device_id=(island_peer(d), shard), device_id_type=MESH)
    for d in range(1, m):
        pl.semaphore_signal(
            barrier, inc=1, device_id=(me, lax.rem(shard + d, m)), device_id_type=MESH
        )
    forward = (table_ref[0], table_ref[1])
    backward = (table_ref[2], table_ref[3])

    in_unit = iota((units, sel_row_ref.shape[1]), 0) == lax.shift_right_logical(sel_row_ref[...], 2)
    lane_block = lax.shift_right_logical(iota((1, width), 1), 6)
    in_lane = (sel_col_ref[...] & 3) == lane_block
    mask = dot(
        jnp.where(in_unit, 1.0, 0.0).astype(BF16), jnp.where(in_lane, 1.0, 0.0).astype(BF16)
    )
    lanes = iota((1, n_blocks), 1)
    block_row = lax.rem(lanes, units) * 4 + lax.div(lanes, units)
    owner_row = owner_row_ref[...]
    earlier = (owner_col_ref[...] == owner_row) & (iota((n_blocks, n_blocks), 0) < block_row)
    slot_row = jnp.sum(jnp.where(earlier, 1, 0), axis=0, keepdims=True)
    held = jnp.where(
        (iota((slots, n_blocks), 0) == slot_row) & (owner_row == me), 1.0, 0.0
    )
    momentum = mom_ref[...]
    previous = jnp.concatenate(
        [
            exact_dot(held[:, j * units : (j + 1) * units], momentum, ((0,), (0,)))
            for j in range(4)
        ],
        axis=1,
    )
    for q in range(n):
        early[q, 0:8] = mask[8 * q : 8 * q + 8]
        early[q, 8:16] = previous[8 * q : 8 * q + 8]

    pl.semaphore_wait(barrier, n + m - 2)

    def early_copy(d):
        return pltpu.make_async_remote_copy(
            src_ref=early.at[island_peer(d)],
            dst_ref=early_in.at[d],
            send_sem=early_send.at[d],
            recv_sem=early_recv.at[d],
            device_id=(island_peer(d), shard),
            device_id_type=MESH,
        )

    def sent_copy(d):
        return pltpu.make_async_remote_copy(
            src_ref=sent.at[island_peer(d)],
            dst_ref=sent_in.at[d],
            send_sem=sent_send.at[d],
            recv_sem=sent_recv.at[d],
            device_id=(island_peer(d), shard),
            device_id_type=MESH,
        )

    def coefs_copy(d, slot):
        return pltpu.make_async_remote_copy(
            src_ref=coefs.at[slot],
            dst_ref=coefs.at[slot],
            send_sem=coefs_send.at[d],
            recv_sem=coefs_recv.at[d],
            device_id=(island_peer(d), shard),
            device_id_type=MESH,
        )

    def squares_copy(d):
        return pltpu.make_async_remote_copy(
            src_ref=squares,
            dst_ref=squares_in.at[d],
            send_sem=squares_send.at[d],
            recv_sem=squares_recv.at[d],
            device_id=(me, lax.rem(shard + d, m)),
            device_id_type=MESH,
        )

    def rows_of(group):
        return pl.ds(pl.multiple_of(group * TILE, TILE), TILE)

    def units_of(group):
        return pl.ds(pl.multiple_of(group * 8, 8), 8)

    def summed(group, half):
        cols = pl.ds(half * TILE, TILE)
        return grad_ref[rows_of(group), cols].astype(F32) + err_ref[rows_of(group), cols].astype(F32)

    @pl.loop(1, n)
    def _(d):
        early_copy(d).start()

    def pick_group(group):
        positions = index_ref[units_of(group), :]
        picked = [None] * 8
        for half in range(2):
            middle = times_table(split(summed(group, half)), backward)
            spectrum = table_times(forward, split(middle))
            for strip in range(4):
                unit = 2 * strip + half
                picked[unit] = gather_unit(
                    spectrum[strip * 64 : strip * 64 + 64], positions[unit : unit + 1]
                )
        sent[group] = jnp.concatenate(picked, axis=0) * early[group, 0:8]

    @pl.loop(1, n)
    def _(d):
        pick_group(island_peer(d))
        sent_copy(d).start()

    pick_group(me)

    def error_group(group):
        positions = index_ref[units_of(group), :]
        values = sent[group]
        for half in range(2):
            rebuilt = decode_tile(values, positions, half, forward, backward)
            new_err_ref[rows_of(group), pl.ds(half * TILE, TILE)] = (
                summed(group, half) - rebuilt
            ).astype(BF16)

    @pl.loop(0, n // 2)
    def _(group):
        error_group(group)

    @pl.loop(1, n)
    def _(d):
        early_copy(d).wait_recv()
        sent_copy(d).wait_recv()

    totals = sent[me]
    counts = early[me, 0:8]
    owned = early[me, 8:16]
    for d in range(1, n):
        totals += sent_in[d]
        counts += early_in[d, 0:8]
        owned += early_in[d, 8:16]
    average = totals / jnp.maximum(counts, 1.0)
    coefs[me] = average + BETA_FACTOR * (BETA_FACTOR * owned + average)

    @pl.loop(1, n)
    def _(d):
        coefs_copy(d, me).start()

    @pl.loop(n // 2, n)
    def _(group):
        error_group(group)

    def update_group(group, total):
        positions = index_ref[units_of(group), :]
        values = coefs[group]
        for half in range(2):
            piece = decode_tile(values, positions, half, forward, backward).astype(BF16)
            update[rows_of(group), pl.ds(half * TILE, TILE)] = piece
            wide = piece.astype(F32)
            total += jnp.sum((wide * wide).reshape(TILE // 8, 8, TILE), axis=0)
        return total

    total = update_group(me, jnp.zeros((8, TILE), F32))

    def arrived(d, total):
        source = island_source(d)
        coefs_copy(d, source).wait_recv()
        return update_group(source, total)

    total = lax.fori_loop(1, n, arrived, total)
    squares[...] = jnp.broadcast_to(jnp.sum(total, keepdims=True), squares.shape)
    for d in range(1, m):
        squares_copy(d).start()

    everything = jnp.concatenate([coefs[q] for q in range(n)], axis=0)
    own = jnp.zeros((slots, kept), F32)
    for j in range(4):
        own += exact_dot(
            held[:, j * units : (j + 1) * units],
            everything[:, j * kept : (j + 1) * kept],
            ((1,), (0,)),
        )
    live = jnp.sum(held, axis=1, keepdims=True)
    own_average = (own - (BETA_FACTOR * BETA_FACTOR) * momentum * live) / (1.0 + BETA_FACTOR)
    new_mom_ref[...] = BETA_FACTOR * momentum + own_average

    for d in range(1, m):
        squares_copy(d).wait_recv()
    total_square = squares[...]
    for d in range(1, m):
        total_square += squares_in[d]
    step = OUTER_RATE / jnp.sqrt(total_square / elements + EPSILON)
    step = step[0:1, 0:1]

    @pl.loop(0, n)
    def _(group):
        new_params_ref[rows_of(group), :] = (
            params_ref[rows_of(group), :].astype(F32) - update[rows_of(group), :].astype(F32) * step
        ).astype(BF16)

    @pl.loop(1, n)
    def _(d):
        early_copy(d).wait_send()
        sent_copy(d).wait_send()
        coefs_copy(d, me).wait_send()

    for d in range(1, m):
        squares_copy(d).wait_send()


def on_device(pseudo_grad, error_buf, params, momentum, sel_blocks, coef_index, owner_map):
    n = lax.axis_size("island")
    m = lax.axis_size("fsdp")
    rows, columns = params.shape
    n_blocks, kept = coef_index.shape
    units = n_blocks // 4
    if rows != n * TILE or columns != 2 * TILE or kept != 64:
        return plain_on_device(
            pseudo_grad, error_buf, params, momentum, sel_blocks, coef_index, owner_map
        )
    slots = momentum.shape[1] // kept
    chunk = (n, 8, TILE)
    vmem = pl.BlockSpec(memory_space=pltpu.VMEM)
    new_params, new_error, new_momentum = pl.pallas_call(
        functools.partial(kernel, n, m, rows * m * columns),
        out_shape=(
            jax.ShapeDtypeStruct((rows, columns), BF16),
            jax.ShapeDtypeStruct((rows, columns), BF16),
            jax.ShapeDtypeStruct((slots, kept), F32),
        ),
        in_specs=[vmem] * 10,
        out_specs=(vmem, vmem, vmem),
        scratch_shapes=[
            pltpu.VMEM((n, 16, TILE), F32),
            pltpu.VMEM((n, 16, TILE), F32),
            pltpu.VMEM(chunk, F32),
            pltpu.VMEM(chunk, F32),
            pltpu.VMEM(chunk, F32),
            pltpu.VMEM((rows, columns), BF16),
            pltpu.VMEM((8, 128), F32),
            pltpu.VMEM((m, 8, 128), F32),
            pltpu.SemaphoreType.DMA((n,)),
            pltpu.SemaphoreType.DMA((n,)),
            pltpu.SemaphoreType.DMA((n,)),
            pltpu.SemaphoreType.DMA((n,)),
            pltpu.SemaphoreType.DMA((n,)),
            pltpu.SemaphoreType.DMA((n,)),
            pltpu.SemaphoreType.DMA((m,)),
            pltpu.SemaphoreType.DMA((m,)),
        ],
        compiler_params=pltpu.CompilerParams(
            collective_id=0, has_side_effects=True, vmem_limit_bytes=48 * 2**20
        ),
        name="outer_step",
    )(
        pseudo_grad[0],
        error_buf[0],
        params,
        momentum.reshape(slots, kept),
        sel_blocks,
        sel_blocks.reshape(-1, 1),
        coef_index.reshape(units, TILE),
        owner_map.reshape(units, 4).T.reshape(1, n_blocks),
        owner_map.reshape(n_blocks, 1),
        jnp.asarray(cosine_parts()),
    )
    return (new_params, new_error[None], new_momentum.reshape(1, slots * kept))


def solution(mesh):
    in_specs = (
        P("island", "fsdp", None),
        P("island", "fsdp", None),
        P("fsdp", None),
        P("island", "fsdp"),
        P("island", "fsdp"),
        P("fsdp", None),
        P("fsdp"),
    )
    out_specs = (P("fsdp", None), P("island", "fsdp", None), P("island", "fsdp"))
    return jax.shard_map(
        on_device, mesh=mesh, in_specs=in_specs, out_specs=out_specs, check_vma=False
    )
```

```python
import functools

import numpy as np

import jax
import jax.numpy as jnp
from jax import lax
from jax.experimental import pallas as pl
from jax.experimental.pallas import tpu as pltpu
from jax.sharding import PartitionSpec as P

BETA_FACTOR = 0.9
OUTER_RATE = 0.5
EPSILON = 1e-06
precise_mode = lax.Precision.HIGHEST


def cosine_table():
    freqs = jnp.arange(64, dtype=jnp.float32)[:, None]
    points = jnp.arange(64, dtype=jnp.float32)[None, :]
    scaling = jnp.where(freqs == 0.0, jnp.sqrt(1.0 / 64.0), jnp.sqrt(2.0 / 64.0))
    return scaling * jnp.cos(jnp.pi * (2.0 * points + 1.0) * freqs / 128.0)


def to_blocks(field):
    row_blocks = field.shape[0] // 64
    col_blocks = field.shape[1] // 64
    return (
        field.reshape(row_blocks, 64, col_blocks, 64)
        .transpose(0, 2, 1, 3)
        .reshape(row_blocks * col_blocks, 64, 64)
    )


def from_blocks(blocks, row_total, col_total):
    row_blocks = row_total // 64
    col_blocks = col_total // 64
    return (
        blocks.reshape(row_blocks, col_blocks, 64, 64)
        .transpose(0, 2, 1, 3)
        .reshape(row_total, col_total)
    )


def forward_blocks(cosine, blocks):
    return jnp.einsum("ij,bjk,lk->bil", cosine, blocks, cosine, precision=precise_mode)


def inverse_blocks(cosine, blocks):
    return jnp.einsum("ji,bjk,kl->bil", cosine, blocks, cosine, precision=precise_mode)


def scatter_coefs(values, positions):
    amount = values.shape[0]
    return (
        jnp.zeros((amount, 4096), jnp.float32)
        .at[jnp.arange(amount)[:, None], positions]
        .set(values)
    )


def plain_on_device(pseudo_grad, error_buf, params, momentum, sel_blocks, coef_index, owner_map):
    cosine = cosine_table()
    islands = lax.axis_size("island")
    my_island = lax.axis_index("island")
    shard_rows = params.shape[0]
    columns = params.shape[1]
    n_blocks = coef_index.shape[0]
    coef_total = coef_index.shape[1]
    capacity = momentum.shape[1] // coef_total
    summed = pseudo_grad[0].astype(jnp.float32) + error_buf[0].astype(jnp.float32)
    blocks = to_blocks(summed)
    spectra = forward_blocks(cosine, blocks).reshape(n_blocks, 4096)
    picked = jnp.take_along_axis(spectra, coef_index, axis=1)
    chosen = sel_blocks[0]
    block_ids = jnp.arange(n_blocks, dtype=jnp.int32)
    chosen_mask = jnp.any(chosen[:, None] == block_ids[None, :], axis=0).astype(jnp.float32)
    outgoing = picked * chosen_mask[:, None]
    rebuilt = inverse_blocks(cosine, scatter_coefs(outgoing, coef_index).reshape(n_blocks, 64, 64))
    new_error = from_blocks(blocks - rebuilt, shard_rows, columns).astype(jnp.bfloat16)[None]
    earlier = (owner_map[None, :] == owner_map[:, None]) & (block_ids[None, :] < block_ids[:, None])
    slot_of = jnp.sum(earlier.astype(jnp.int32), axis=1)
    target = owner_map * capacity + slot_of
    own_slots = my_island * capacity + jnp.arange(capacity, dtype=jnp.int32)
    owned_mask = target[None, :] == own_slots[:, None]
    owned_ids = jnp.sum(jnp.where(owned_mask, block_ids[None, :], 0), axis=1)
    owned_live = jnp.any(owned_mask, axis=1)
    owned_pattern = jnp.sum(jnp.where(owned_mask[:, :, None], coef_index[None, :, :], 0), axis=1)
    listed = outgoing[chosen]
    piece_values = lax.all_gather(listed, "island", axis=0, tiled=True)
    piece_ids = lax.all_gather(chosen, "island", axis=0, tiled=True)
    matches = ((piece_ids[None, :] == owned_ids[:, None]) & owned_live[:, None]).astype(jnp.float32)
    totals = jnp.dot(matches, piece_values, precision=precise_mode)
    counts = jnp.sum(matches, axis=1)
    average = totals / jnp.maximum(counts, 1.0)[:, None]
    previous = momentum[0].reshape(capacity, coef_total)
    refreshed = BETA_FACTOR * previous + average
    update_coef = average + BETA_FACTOR * refreshed
    new_momentum = refreshed.reshape(1, capacity * coef_total)
    owner_dense = inverse_blocks(
        cosine, scatter_coefs(update_coef, owned_pattern).reshape(capacity, 64, 64)
    )
    owner_dense = owner_dense.reshape(capacity, 4096).astype(jnp.bfloat16)
    gathered_dense = lax.all_gather(owner_dense, "island", axis=0, tiled=True)
    selector = (target[:, None] == jnp.arange(islands * capacity, dtype=jnp.int32)[None, :]).astype(
        jnp.bfloat16
    )
    received = jnp.dot(selector, gathered_dense, preferred_element_type=jnp.float32)
    local_square = jnp.sum(received * received)
    total_square = lax.psum(local_square, "fsdp")
    scale_root = jnp.sqrt(total_square / (shard_rows * lax.axis_size("fsdp") * columns) + EPSILON)
    shifted = from_blocks(received.reshape(n_blocks, 64, 64), shard_rows, columns)
    new_params = (params.astype(jnp.float32) - OUTER_RATE * shifted / scale_root).astype(
        jnp.bfloat16
    )
    return (new_params, new_error, new_momentum)


MESH = pl.DeviceIdType.MESH
TILE = 256
F32 = jnp.float32
BF16 = jnp.bfloat16


def cosine_parts():
    freqs = np.arange(64)[:, None]
    points = np.arange(64)[None, :]
    scaling = np.where(freqs == 0, np.sqrt(1.0 / 64.0), np.sqrt(2.0 / 64.0))
    cosine = scaling * np.cos(np.pi * (2.0 * points + 1.0) * freqs / 128.0)
    diagonal = np.kron(np.eye(4), cosine).astype(np.float32)
    parts = []
    for table in (diagonal, diagonal.T):
        high = table.astype(BF16)
        parts += [high, (table - high.astype(np.float32)).astype(BF16)]
    return np.stack(parts)


def iota(shape, dim):
    return lax.broadcasted_iota(jnp.int32, shape, dim)


def split(value):
    high = value.astype(BF16)
    return high, (value - high.astype(F32)).astype(BF16)


def dot(a, b):
    return jnp.dot(a, b, preferred_element_type=F32)


def exact_dot(a, b, dims):
    return lax.dot_general(
        a, b, (dims, ((), ())), precision=precise_mode, preferred_element_type=F32
    )


def times_table(parts, table_ref, which):
    rows = parts[0].shape[0]
    both = dot(jnp.concatenate(parts, axis=0), table_ref[which])
    return both[:rows] + both[rows:] + dot(parts[0], table_ref[which + 1])


def table_times(table_ref, which, parts):
    stacked = table_ref[which : which + 2].reshape(2 * TILE, TILE)
    both = dot(stacked, parts[0])
    return both[:TILE] + both[TILE:] + dot(table_ref[which], parts[1])


def row_mask_of(positions):
    return iota((64, TILE), 0) == lax.shift_right_logical(positions, 6)


def col_mask_of(positions):
    cols = (positions & 63) + (iota((1, TILE), 1) & -64)
    rows = iota((TILE, TILE), 0).astype(F32).astype(BF16)
    here = rows == cols.astype(F32).astype(BF16)
    return jnp.where(here, jnp.ones((), BF16), jnp.zeros((), BF16))


def gather_unit(spectrum, positions, col_mask):
    both = dot(jnp.concatenate(split(spectrum), axis=0), col_mask)
    return jnp.sum(
        jnp.where(row_mask_of(positions), both[:64] + both[64:], 0.0), axis=0, keepdims=True
    )


def scatter_unit(parts, col_mask):
    return lax.dot_general(
        jnp.concatenate(parts, axis=0),
        col_mask,
        (((1,), (1,)), ((), ())),
        preferred_element_type=F32,
    ).astype(BF16)


def decode_tile(values, positions, masks_ref, first, half, table_ref):
    highs, lows = [], []
    for strip in range(4):
        unit = 2 * strip + half
        placed = jnp.where(row_mask_of(positions[unit : unit + 1]), values[unit : unit + 1], 0.0)
        both = scatter_unit(split(placed), masks_ref[first + unit])
        highs.append(both[:64])
        lows.append(both[64:])
    parts = (jnp.concatenate(highs, axis=0), jnp.concatenate(lows, axis=0))
    return table_times(table_ref, 2, split(times_table(parts, table_ref, 0)))


def decode_tile_short(values, positions, masks_ref, first, half, table_ref):
    pieces = []
    for strip in range(4):
        unit = 2 * strip + half
        placed = jnp.where(row_mask_of(positions[unit : unit + 1]), values[unit : unit + 1], 0.0)
        pieces.append(scatter_unit([placed.astype(BF16)], masks_ref[first + unit]))
    middle = dot(jnp.concatenate(pieces, axis=0), table_ref[0]).astype(BF16)
    return dot(table_ref[2], middle)


def kernel(
    n,
    m,
    elements,
    grad_ref,
    err_ref,
    mom_ref,
    sel_row_ref,
    sel_col_ref,
    index_ref,
    owner_row_ref,
    owner_col_ref,
    table_ref,
    update,
    new_err_ref,
    new_mom_ref,
    step_ref,
    masks,
    early,
    early_in,
    sent,
    sent_in,
    coefs,
    squares,
    squares_in,
    early_send,
    early_recv,
    sent_send,
    sent_recv,
    coefs_send,
    coefs_recv,
    squares_send,
    squares_recv,
):
    me = lax.axis_index("island")
    shard = lax.axis_index("fsdp")
    units, width = index_ref.shape
    slots, kept = mom_ref.shape
    n_blocks = owner_col_ref.shape[0]

    def island_peer(d):
        return lax.rem(me + d, n)

    def island_source(d):
        return lax.rem(me - d + n, n)

    barrier = pltpu.get_barrier_semaphore()
    for d in range(1, n):
        pl.semaphore_signal(barrier, inc=1, device_id=(island_peer(d), shard), device_id_type=MESH)
    for d in range(1, m):
        pl.semaphore_signal(
            barrier, inc=1, device_id=(me, lax.rem(shard + d, m)), device_id_type=MESH
        )

    in_unit = iota((units, sel_row_ref.shape[1]), 0) == lax.shift_right_logical(sel_row_ref[...], 2)
    lane_block = lax.shift_right_logical(iota((1, width), 1), 6)
    in_lane = (sel_col_ref[...] & 3) == lane_block
    mask = dot(
        jnp.where(in_unit, 1.0, 0.0).astype(BF16), jnp.where(in_lane, 1.0, 0.0).astype(BF16)
    )
    lanes = iota((1, n_blocks), 1)
    block_row = lax.rem(lanes, units) * 4 + lax.div(lanes, units)
    owner_row = owner_row_ref[...]
    earlier = (owner_col_ref[...] == owner_row) & (iota((n_blocks, n_blocks), 0) < block_row)
    slot_row = jnp.sum(jnp.where(earlier, 1, 0), axis=0, keepdims=True)
    held = jnp.where(
        (iota((slots, n_blocks), 0) == slot_row) & (owner_row == me), 1.0, 0.0
    )
    momentum = mom_ref[...]
    previous = jnp.concatenate(
        [
            exact_dot(held[:, j * units : (j + 1) * units], momentum, ((0,), (0,)))
            for j in range(4)
        ],
        axis=1,
    )
    for q in range(n):
        early[q, 0:8] = mask[8 * q : 8 * q + 8]
        early[q, 8:16] = previous[8 * q : 8 * q + 8]

    pl.semaphore_wait(barrier, n + m - 2)

    def early_copy(d):
        return pltpu.make_async_remote_copy(
            src_ref=early.at[island_peer(d)],
            dst_ref=early_in.at[d],
            send_sem=early_send.at[d],
            recv_sem=early_recv.at[d],
            device_id=(island_peer(d), shard),
            device_id_type=MESH,
        )

    def sent_copy(d):
        return pltpu.make_async_remote_copy(
            src_ref=sent.at[island_peer(d)],
            dst_ref=sent_in.at[d],
            send_sem=sent_send.at[d],
            recv_sem=sent_recv.at[d],
            device_id=(island_peer(d), shard),
            device_id_type=MESH,
        )

    def coefs_copy(d, slot):
        return pltpu.make_async_remote_copy(
            src_ref=coefs.at[slot],
            dst_ref=coefs.at[slot],
            send_sem=coefs_send.at[d],
            recv_sem=coefs_recv.at[d],
            device_id=(island_peer(d), shard),
            device_id_type=MESH,
        )

    def squares_copy(d):
        return pltpu.make_async_remote_copy(
            src_ref=squares,
            dst_ref=squares_in.at[d],
            send_sem=squares_send.at[d],
            recv_sem=squares_recv.at[d],
            device_id=(me, lax.rem(shard + d, m)),
            device_id_type=MESH,
        )

    def rows_of(group):
        return pl.ds(pl.multiple_of(group * TILE, TILE), TILE)

    def units_of(group):
        return pl.ds(pl.multiple_of(group * 8, 8), 8)

    def summed(group, half):
        cols = pl.ds(half * TILE, TILE)
        return grad_ref[rows_of(group), cols].astype(F32) + err_ref[rows_of(group), cols].astype(F32)

    @pl.loop(1, n)
    def _(d):
        early_copy(d).start()

    def pick_group(group):
        positions = index_ref[units_of(group), :]
        picked = [None] * 8
        for half in range(2):
            middle = times_table(split(summed(group, half)), table_ref, 2)
            spectrum = table_times(table_ref, 0, split(middle))
            for strip in range(4):
                unit = 2 * strip + half
                col_mask = col_mask_of(positions[unit : unit + 1])
                masks[group * 8 + unit] = col_mask
                picked[unit] = gather_unit(
                    spectrum[strip * 64 : strip * 64 + 64], positions[unit : unit + 1], col_mask
                )
        sent[group] = jnp.concatenate(picked, axis=0) * early[group, 0:8]

    @pl.loop(1, n)
    def _(d):
        pick_group(island_peer(d))
        sent_copy(d).start()

    pick_group(me)

    def error_group(group):
        positions = index_ref[units_of(group), :]
        values = sent[group]
        for half in range(2):
            rebuilt = decode_tile_short(values, positions, masks, group * 8, half, table_ref)
            new_err_ref[rows_of(group), pl.ds(half * TILE, TILE)] = (
                summed(group, half) - rebuilt
            ).astype(BF16)

    @pl.loop(0, n // 2)
    def _(group):
        error_group(group)

    @pl.loop(1, n)
    def _(d):
        early_copy(d).wait_recv()
        sent_copy(d).wait_recv()

    totals = sent[me]
    counts = early[me, 0:8]
    owned = early[me, 8:16]
    for d in range(1, n):
        totals += sent_in[d]
        counts += early_in[d, 0:8]
        owned += early_in[d, 8:16]
    average = totals / jnp.maximum(counts, 1.0)
    coefs[me] = average + BETA_FACTOR * (BETA_FACTOR * owned + average)

    @pl.loop(1, n)
    def _(d):
        coefs_copy(d, me).start()

    @pl.loop(n // 2, n)
    def _(group):
        error_group(group)

    def update_group(group, total):
        positions = index_ref[units_of(group), :]
        values = coefs[group]
        for half in range(2):
            piece = decode_tile(values, positions, masks, group * 8, half, table_ref).astype(BF16)
            update[rows_of(group), pl.ds(half * TILE, TILE)] = piece
            wide = piece.astype(F32)
            total += jnp.sum((wide * wide).reshape(TILE // 8, 8, TILE), axis=0)
        return total

    total = update_group(me, jnp.zeros((8, TILE), F32))

    def arrived(d, total):
        source = island_source(d)
        coefs_copy(d, source).wait_recv()
        return update_group(source, total)

    total = lax.fori_loop(1, n, arrived, total)
    squares[...] = jnp.broadcast_to(jnp.sum(total, keepdims=True), squares.shape)
    for d in range(1, m):
        squares_copy(d).start()

    everything = jnp.concatenate([coefs[q] for q in range(n)], axis=0)
    own = jnp.zeros((slots, kept), F32)
    for j in range(4):
        own += exact_dot(
            held[:, j * units : (j + 1) * units],
            everything[:, j * kept : (j + 1) * kept],
            ((1,), (0,)),
        )
    live = jnp.sum(held, axis=1, keepdims=True)
    own_average = (own - (BETA_FACTOR * BETA_FACTOR) * momentum * live) / (1.0 + BETA_FACTOR)
    new_mom_ref[...] = BETA_FACTOR * momentum + own_average

    for d in range(1, m):
        squares_copy(d).wait_recv()
    total_square = squares[...]
    for d in range(1, m):
        total_square += squares_in[d]
    step_ref[...] = OUTER_RATE / jnp.sqrt(total_square / elements + EPSILON)

    @pl.loop(1, n)
    def _(d):
        early_copy(d).wait_send()
        sent_copy(d).wait_send()
        coefs_copy(d, me).wait_send()

    for d in range(1, m):
        squares_copy(d).wait_send()


def on_device(pseudo_grad, error_buf, params, momentum, sel_blocks, coef_index, owner_map):
    n = lax.axis_size("island")
    m = lax.axis_size("fsdp")
    rows, columns = params.shape
    n_blocks, kept = coef_index.shape
    units = n_blocks // 4
    if rows != n * TILE or columns != 2 * TILE or kept != 64:
        return plain_on_device(
            pseudo_grad, error_buf, params, momentum, sel_blocks, coef_index, owner_map
        )
    slots = momentum.shape[1] // kept
    chunk = (n, 8, TILE)
    vmem = pl.BlockSpec(memory_space=pltpu.VMEM)
    update, new_error, new_momentum, step = pl.pallas_call(
        functools.partial(kernel, n, m, rows * m * columns),
        out_shape=(
            jax.ShapeDtypeStruct((rows, columns), BF16),
            jax.ShapeDtypeStruct((rows, columns), BF16),
            jax.ShapeDtypeStruct((slots, kept), F32),
            jax.ShapeDtypeStruct((8, 128), F32),
        ),
        in_specs=[vmem] * 9,
        out_specs=(vmem,) * 4,
        scratch_shapes=[
            pltpu.VMEM((units, TILE, TILE), BF16),
            pltpu.VMEM((n, 16, TILE), F32),
            pltpu.VMEM((n, 16, TILE), F32),
            pltpu.VMEM(chunk, F32),
            pltpu.VMEM(chunk, F32),
            pltpu.VMEM(chunk, F32),
            pltpu.VMEM((8, 128), F32),
            pltpu.VMEM((m, 8, 128), F32),
            pltpu.SemaphoreType.DMA((n,)),
            pltpu.SemaphoreType.DMA((n,)),
            pltpu.SemaphoreType.DMA((n,)),
            pltpu.SemaphoreType.DMA((n,)),
            pltpu.SemaphoreType.DMA((n,)),
            pltpu.SemaphoreType.DMA((n,)),
            pltpu.SemaphoreType.DMA((m,)),
            pltpu.SemaphoreType.DMA((m,)),
        ],
        compiler_params=pltpu.CompilerParams(
            collective_id=0, has_side_effects=True, vmem_limit_bytes=48 * 2**20
        ),
        name="outer_step",
    )(
        pseudo_grad[0],
        error_buf[0],
        momentum.reshape(slots, kept),
        sel_blocks,
        sel_blocks.reshape(-1, 1),
        coef_index.reshape(units, TILE),
        owner_map.reshape(units, 4).T.reshape(1, n_blocks),
        owner_map.reshape(n_blocks, 1),
        jnp.asarray(cosine_parts()),
    )
    new_params = (params.astype(F32) - update.astype(F32) * step[0, 0]).astype(BF16)
    return (new_params, new_error[None], new_momentum.reshape(1, slots * kept))


def solution(mesh):
    in_specs = (
        P("island", "fsdp", None),
        P("island", "fsdp", None),
        P("fsdp", None),
        P("island", "fsdp"),
        P("island", "fsdp"),
        P("fsdp", None),
        P("fsdp"),
    )
    out_specs = (P("fsdp", None), P("island", "fsdp", None), P("island", "fsdp"))
    return jax.shard_map(
        on_device, mesh=mesh, in_specs=in_specs, out_specs=out_specs, check_vma=False
    )
```

```python
import functools

import numpy as np

import jax
import jax.numpy as jnp
from jax import lax
from jax.experimental import pallas as pl
from jax.experimental.pallas import tpu as pltpu
from jax.sharding import PartitionSpec as P

BETA_FACTOR = 0.9
OUTER_RATE = 0.5
EPSILON = 1e-06
precise_mode = lax.Precision.HIGHEST


def cosine_table():
    freqs = jnp.arange(64, dtype=jnp.float32)[:, None]
    points = jnp.arange(64, dtype=jnp.float32)[None, :]
    scaling = jnp.where(freqs == 0.0, jnp.sqrt(1.0 / 64.0), jnp.sqrt(2.0 / 64.0))
    return scaling * jnp.cos(jnp.pi * (2.0 * points + 1.0) * freqs / 128.0)


def to_blocks(field):
    row_blocks = field.shape[0] // 64
    col_blocks = field.shape[1] // 64
    return (
        field.reshape(row_blocks, 64, col_blocks, 64)
        .transpose(0, 2, 1, 3)
        .reshape(row_blocks * col_blocks, 64, 64)
    )


def from_blocks(blocks, row_total, col_total):
    row_blocks = row_total // 64
    col_blocks = col_total // 64
    return (
        blocks.reshape(row_blocks, col_blocks, 64, 64)
        .transpose(0, 2, 1, 3)
        .reshape(row_total, col_total)
    )


def forward_blocks(cosine, blocks):
    return jnp.einsum("ij,bjk,lk->bil", cosine, blocks, cosine, precision=precise_mode)


def inverse_blocks(cosine, blocks):
    return jnp.einsum("ji,bjk,kl->bil", cosine, blocks, cosine, precision=precise_mode)


def scatter_coefs(values, positions):
    amount = values.shape[0]
    return (
        jnp.zeros((amount, 4096), jnp.float32)
        .at[jnp.arange(amount)[:, None], positions]
        .set(values)
    )


def plain_on_device(pseudo_grad, error_buf, params, momentum, sel_blocks, coef_index, owner_map):
    cosine = cosine_table()
    islands = lax.axis_size("island")
    my_island = lax.axis_index("island")
    shard_rows = params.shape[0]
    columns = params.shape[1]
    n_blocks = coef_index.shape[0]
    coef_total = coef_index.shape[1]
    capacity = momentum.shape[1] // coef_total
    summed = pseudo_grad[0].astype(jnp.float32) + error_buf[0].astype(jnp.float32)
    blocks = to_blocks(summed)
    spectra = forward_blocks(cosine, blocks).reshape(n_blocks, 4096)
    picked = jnp.take_along_axis(spectra, coef_index, axis=1)
    chosen = sel_blocks[0]
    block_ids = jnp.arange(n_blocks, dtype=jnp.int32)
    chosen_mask = jnp.any(chosen[:, None] == block_ids[None, :], axis=0).astype(jnp.float32)
    outgoing = picked * chosen_mask[:, None]
    rebuilt = inverse_blocks(cosine, scatter_coefs(outgoing, coef_index).reshape(n_blocks, 64, 64))
    new_error = from_blocks(blocks - rebuilt, shard_rows, columns).astype(jnp.bfloat16)[None]
    earlier = (owner_map[None, :] == owner_map[:, None]) & (block_ids[None, :] < block_ids[:, None])
    slot_of = jnp.sum(earlier.astype(jnp.int32), axis=1)
    target = owner_map * capacity + slot_of
    own_slots = my_island * capacity + jnp.arange(capacity, dtype=jnp.int32)
    owned_mask = target[None, :] == own_slots[:, None]
    owned_ids = jnp.sum(jnp.where(owned_mask, block_ids[None, :], 0), axis=1)
    owned_live = jnp.any(owned_mask, axis=1)
    owned_pattern = jnp.sum(jnp.where(owned_mask[:, :, None], coef_index[None, :, :], 0), axis=1)
    listed = outgoing[chosen]
    piece_values = lax.all_gather(listed, "island", axis=0, tiled=True)
    piece_ids = lax.all_gather(chosen, "island", axis=0, tiled=True)
    matches = ((piece_ids[None, :] == owned_ids[:, None]) & owned_live[:, None]).astype(jnp.float32)
    totals = jnp.dot(matches, piece_values, precision=precise_mode)
    counts = jnp.sum(matches, axis=1)
    average = totals / jnp.maximum(counts, 1.0)[:, None]
    previous = momentum[0].reshape(capacity, coef_total)
    refreshed = BETA_FACTOR * previous + average
    update_coef = average + BETA_FACTOR * refreshed
    new_momentum = refreshed.reshape(1, capacity * coef_total)
    owner_dense = inverse_blocks(
        cosine, scatter_coefs(update_coef, owned_pattern).reshape(capacity, 64, 64)
    )
    owner_dense = owner_dense.reshape(capacity, 4096).astype(jnp.bfloat16)
    gathered_dense = lax.all_gather(owner_dense, "island", axis=0, tiled=True)
    selector = (target[:, None] == jnp.arange(islands * capacity, dtype=jnp.int32)[None, :]).astype(
        jnp.bfloat16
    )
    received = jnp.dot(selector, gathered_dense, preferred_element_type=jnp.float32)
    local_square = jnp.sum(received * received)
    total_square = lax.psum(local_square, "fsdp")
    scale_root = jnp.sqrt(total_square / (shard_rows * lax.axis_size("fsdp") * columns) + EPSILON)
    shifted = from_blocks(received.reshape(n_blocks, 64, 64), shard_rows, columns)
    new_params = (params.astype(jnp.float32) - OUTER_RATE * shifted / scale_root).astype(
        jnp.bfloat16
    )
    return (new_params, new_error, new_momentum)


MESH = pl.DeviceIdType.MESH
TILE = 256
F32 = jnp.float32
BF16 = jnp.bfloat16


def cosine_parts():
    freqs = np.arange(64)[:, None]
    points = np.arange(64)[None, :]
    scaling = np.where(freqs == 0, np.sqrt(1.0 / 64.0), np.sqrt(2.0 / 64.0))
    cosine = scaling * np.cos(np.pi * (2.0 * points + 1.0) * freqs / 128.0)
    cosine = cosine.astype(np.float32)
    parts = []
    for table in (np.tile(cosine, (1, 4)), np.tile(cosine.T, (1, 4))):
        high = table.astype(BF16)
        parts += [high, (table - high.astype(np.float32)).astype(BF16)]
    return np.stack(parts)


def iota(shape, dim):
    return lax.broadcasted_iota(jnp.int32, shape, dim)


def split(value):
    high = value.astype(BF16)
    return high, (value - high.astype(F32)).astype(BF16)


def dot(a, b):
    return jnp.dot(a, b, preferred_element_type=F32)


def exact_dot(a, b, dims):
    return lax.dot_general(
        a, b, (dims, ((), ())), precision=precise_mode, preferred_element_type=F32
    )


def times_table(parts, table_ref, which):
    rows = parts[0].shape[0]
    both = dot(jnp.concatenate(parts, axis=0), table_ref[which])
    return both[:rows] + both[rows:] + dot(parts[0], table_ref[which + 1])


def table_times(table_ref, which, parts):
    stacked = table_ref[which : which + 2].reshape(2 * TILE, TILE)
    both = dot(stacked, parts[0])
    return both[:TILE] + both[TILE:] + dot(table_ref[which], parts[1])


def row_mask_of(positions):
    return iota((64, TILE), 0) == lax.shift_right_logical(positions, 6)


def col_mask_of(positions):
    cols = (positions & 63) + (iota((1, TILE), 1) & -64)
    rows = iota((TILE, TILE), 0).astype(F32).astype(BF16)
    here = rows == cols.astype(F32).astype(BF16)
    return jnp.where(here, jnp.ones((), BF16), jnp.zeros((), BF16))


def gather_unit(spectrum, positions, col_mask):
    both = dot(jnp.concatenate(split(spectrum), axis=0), col_mask)
    return jnp.sum(
        jnp.where(row_mask_of(positions), both[:64] + both[64:], 0.0), axis=0, keepdims=True
    )


def scatter_unit(parts, col_mask):
    return lax.dot_general(
        jnp.concatenate(parts, axis=0),
        col_mask,
        (((1,), (1,)), ((), ())),
        preferred_element_type=F32,
    ).astype(BF16)


def decode_tile(values, positions, masks_ref, first, half, table_ref):
    highs, lows = [], []
    for strip in range(4):
        unit = 2 * strip + half
        placed = jnp.where(row_mask_of(positions[unit : unit + 1]), values[unit : unit + 1], 0.0)
        both = scatter_unit(split(placed), masks_ref[first + unit])
        highs.append(both[:64])
        lows.append(both[64:])
    parts = (jnp.concatenate(highs, axis=0), jnp.concatenate(lows, axis=0))
    return table_times(table_ref, 2, split(times_table(parts, table_ref, 0)))


def decode_tile_short(values, positions, masks_ref, first, half, table_ref):
    pieces = []
    for strip in range(4):
        unit = 2 * strip + half
        placed = jnp.where(row_mask_of(positions[unit : unit + 1]), values[unit : unit + 1], 0.0)
        pieces.append(scatter_unit([placed.astype(BF16)], masks_ref[first + unit]))
    middle = dot(jnp.concatenate(pieces, axis=0), table_ref[0]).astype(BF16)
    return dot(table_ref[2], middle)


def column_of(row):
    extent = row.shape[1]
    diagonal = iota((extent, extent), 0) == iota((extent, extent), 1)
    column = jnp.sum(jnp.where(diagonal, row.astype(F32), 0.0), axis=1, keepdims=True)
    return column.astype(jnp.int32)


def kernel(
    n,
    m,
    elements,
    grad_hbm,
    err_hbm,
    mom_ref,
    sel_ref,
    index_ref,
    owner_ref,
    cosine_ref,
    update,
    new_err_ref,
    new_mom_ref,
    step_ref,
    grad_ref,
    err_ref,
    table_ref,
    masks,
    early,
    early_in,
    sent,
    sent_in,
    coefs,
    squares,
    squares_in,
    early_send,
    early_recv,
    sent_send,
    sent_recv,
    coefs_send,
    coefs_recv,
    squares_send,
    squares_recv,
    load_sem,
):
    me = lax.axis_index("island")
    shard = lax.axis_index("fsdp")
    units, width = index_ref.shape
    kept = 64
    slots = mom_ref.shape[1] // kept
    pairs = slots // 2
    n_blocks = owner_ref.shape[1]
    load_grad = pltpu.make_async_copy(grad_hbm, grad_ref, load_sem.at[0])
    load_err = pltpu.make_async_copy(err_hbm, err_ref, load_sem.at[1])
    load_grad.start()
    load_err.start()

    def island_peer(d):
        return lax.rem(me + d, n)

    def island_source(d):
        return lax.rem(me - d + n, n)

    barrier = pltpu.get_barrier_semaphore()
    for d in range(1, n):
        pl.semaphore_signal(barrier, inc=1, device_id=(island_peer(d), shard), device_id_type=MESH)
    for d in range(1, m):
        pl.semaphore_signal(
            barrier, inc=1, device_id=(me, lax.rem(shard + d, m)), device_id_type=MESH
        )

    lane_block = lax.shift_right_logical(iota((1, width), 1), 6)
    for q in range(4):
        keep = jnp.where(lane_block == q, 1.0, 0.0).astype(BF16)
        for which in range(4):
            table_ref[which, q * 64 : q * 64 + 64] = cosine_ref[which] * keep

    sel_row = sel_ref[...]
    sel_col = column_of(sel_row)
    in_unit = iota((units, sel_row.shape[1]), 0) == lax.shift_right_logical(sel_row, 2)
    in_lane = (sel_col & 3) == lane_block
    mask = dot(
        jnp.where(in_unit, 1.0, 0.0).astype(BF16), jnp.where(in_lane, 1.0, 0.0).astype(BF16)
    )
    owner_row = owner_ref[...]
    earlier = (column_of(owner_row) == owner_row) & (
        iota((n_blocks, n_blocks), 0) < iota((n_blocks, n_blocks), 1)
    )
    slot_row = jnp.sum(jnp.where(earlier, 1, 0), axis=0, keepdims=True)
    place = iota((slots, n_blocks), 0)
    slot_at = jnp.where(place < pairs, 2 * place, 2 * (place - pairs) + 1)
    held = jnp.where((slot_at == slot_row) & (owner_row == me), 1.0, 0.0)
    paired = jnp.concatenate([mom_ref[0:1, p * 128 : p * 128 + 128] for p in range(pairs)], axis=0)
    momentum = jnp.concatenate([paired[:, :kept], paired[:, kept:]], axis=0)
    unit_of = jnp.where(
        iota((units, n_blocks), 0) == lax.shift_right_logical(iota((units, n_blocks), 1), 2),
        1.0,
        0.0,
    )
    in_place = (iota((n_blocks, width), 0) & 3) == lane_block
    by_block = exact_dot(held, jnp.concatenate([momentum] * 4, axis=1), ((0,), (0,)))
    previous = exact_dot(unit_of, jnp.where(in_place, by_block, 0.0), ((1,), (0,)))
    for q in range(n):
        early[q, 0:8] = mask[8 * q : 8 * q + 8]
        early[q, 8:16] = previous[8 * q : 8 * q + 8]

    pl.semaphore_wait(barrier, n + m - 2)

    def early_copy(d):
        return pltpu.make_async_remote_copy(
            src_ref=early.at[island_peer(d)],
            dst_ref=early_in.at[d],
            send_sem=early_send.at[d],
            recv_sem=early_recv.at[d],
            device_id=(island_peer(d), shard),
            device_id_type=MESH,
        )

    def sent_copy(d):
        return pltpu.make_async_remote_copy(
            src_ref=sent.at[island_peer(d)],
            dst_ref=sent_in.at[d],
            send_sem=sent_send.at[d],
            recv_sem=sent_recv.at[d],
            device_id=(island_peer(d), shard),
            device_id_type=MESH,
        )

    def coefs_copy(d, slot):
        return pltpu.make_async_remote_copy(
            src_ref=coefs.at[slot],
            dst_ref=coefs.at[slot],
            send_sem=coefs_send.at[d],
            recv_sem=coefs_recv.at[d],
            device_id=(island_peer(d), shard),
            device_id_type=MESH,
        )

    def squares_copy(d):
        return pltpu.make_async_remote_copy(
            src_ref=squares,
            dst_ref=squares_in.at[d],
            send_sem=squares_send.at[d],
            recv_sem=squares_recv.at[d],
            device_id=(me, lax.rem(shard + d, m)),
            device_id_type=MESH,
        )

    def rows_of(group):
        return pl.ds(pl.multiple_of(group * TILE, TILE), TILE)

    def units_of(group):
        return pl.ds(pl.multiple_of(group * 8, 8), 8)

    def summed(group, half):
        cols = pl.ds(half * TILE, TILE)
        return grad_ref[rows_of(group), cols].astype(F32) + err_ref[rows_of(group), cols].astype(F32)

    @pl.loop(1, n)
    def _(d):
        early_copy(d).start()

    load_grad.wait()
    load_err.wait()

    def pick_group(group):
        positions = index_ref[units_of(group), :]
        picked = [None] * 8
        for half in range(2):
            middle = times_table(split(summed(group, half)), table_ref, 2)
            spectrum = table_times(table_ref, 0, split(middle))
            for strip in range(4):
                unit = 2 * strip + half
                col_mask = col_mask_of(positions[unit : unit + 1])
                masks[group * 8 + unit] = col_mask
                picked[unit] = gather_unit(
                    spectrum[strip * 64 : strip * 64 + 64], positions[unit : unit + 1], col_mask
                )
        sent[group] = jnp.concatenate(picked, axis=0) * early[group, 0:8]

    @pl.loop(1, n)
    def _(d):
        pick_group(island_peer(d))
        sent_copy(d).start()

    pick_group(me)

    def error_group(group):
        positions = index_ref[units_of(group), :]
        values = sent[group]
        for half in range(2):
            rebuilt = decode_tile_short(values, positions, masks, group * 8, half, table_ref)
            new_err_ref[rows_of(group), pl.ds(half * TILE, TILE)] = (
                summed(group, half) - rebuilt
            ).astype(BF16)

    @pl.loop(0, n // 2)
    def _(group):
        error_group(group)

    @pl.loop(1, n)
    def _(d):
        early_copy(d).wait_recv()
        sent_copy(d).wait_recv()

    totals = sent[me]
    counts = early[me, 0:8]
    owned = early[me, 8:16]
    for d in range(1, n):
        totals += sent_in[d]
        counts += early_in[d, 0:8]
        owned += early_in[d, 8:16]
    average = totals / jnp.maximum(counts, 1.0)
    coefs[me] = average + BETA_FACTOR * (BETA_FACTOR * owned + average)

    @pl.loop(1, n)
    def _(d):
        coefs_copy(d, me).start()

    @pl.loop(n // 2, n)
    def _(group):
        error_group(group)

    def update_group(group, total):
        positions = index_ref[units_of(group), :]
        values = coefs[group]
        for half in range(2):
            piece = decode_tile(values, positions, masks, group * 8, half, table_ref).astype(BF16)
            update[rows_of(group), pl.ds(half * TILE, TILE)] = piece
            wide = piece.astype(F32)
            total += jnp.sum((wide * wide).reshape(TILE // 8, 8, TILE), axis=0)
        return total

    total = update_group(me, jnp.zeros((8, TILE), F32))

    def arrived(d, total):
        source = island_source(d)
        coefs_copy(d, source).wait_recv()
        return update_group(source, total)

    total = lax.fori_loop(1, n, arrived, total)
    squares[...] = jnp.broadcast_to(jnp.sum(total, keepdims=True), squares.shape)
    for d in range(1, m):
        squares_copy(d).start()

    everything = jnp.concatenate([coefs[q] for q in range(n)], axis=0)
    by_block = exact_dot(unit_of, everything, ((0,), (0,)))
    wide_own = exact_dot(held, jnp.where(in_place, by_block, 0.0), ((1,), (0,)))
    own = wide_own[:, :kept]
    for j in range(1, 4):
        own += wide_own[:, j * kept : (j + 1) * kept]
    live = jnp.sum(held, axis=1, keepdims=True)
    own_average = (own - (BETA_FACTOR * BETA_FACTOR) * momentum * live) / (1.0 + BETA_FACTOR)
    refreshed = BETA_FACTOR * momentum + own_average
    refreshed = jnp.concatenate([refreshed[:pairs], refreshed[pairs:]], axis=1)
    for p in range(pairs):
        new_mom_ref[0:1, p * 128 : p * 128 + 128] = refreshed[p : p + 1]

    for d in range(1, m):
        squares_copy(d).wait_recv()
    total_square = squares[...]
    for d in range(1, m):
        total_square += squares_in[d]
    step_ref[...] = OUTER_RATE / jnp.sqrt(total_square / elements + EPSILON)

    @pl.loop(1, n)
    def _(d):
        early_copy(d).wait_send()
        sent_copy(d).wait_send()
        coefs_copy(d, me).wait_send()

    for d in range(1, m):
        squares_copy(d).wait_send()


def on_device(pseudo_grad, error_buf, params, momentum, sel_blocks, coef_index, owner_map):
    n = lax.axis_size("island")
    m = lax.axis_size("fsdp")
    rows, columns = params.shape
    n_blocks, kept = coef_index.shape
    units = n_blocks // 4
    if rows != n * TILE or columns != 2 * TILE or kept != 64 or momentum.shape[1] % 128:
        return plain_on_device(
            pseudo_grad, error_buf, params, momentum, sel_blocks, coef_index, owner_map
        )
    slots = momentum.shape[1] // kept
    chunk = (n, 8, TILE)
    vmem = pl.BlockSpec(memory_space=pltpu.VMEM)
    update, new_error, new_momentum, step = pl.pallas_call(
        functools.partial(kernel, n, m, rows * m * columns),
        out_shape=(
            jax.ShapeDtypeStruct((rows, columns), BF16),
            jax.ShapeDtypeStruct((rows, columns), BF16),
            jax.ShapeDtypeStruct((1, slots * kept), F32),
            jax.ShapeDtypeStruct((8, 128), F32),
        ),
        in_specs=[pl.BlockSpec(memory_space=pl.ANY)] * 2 + [vmem] * 5,
        out_specs=(vmem,) * 4,
        scratch_shapes=[
            pltpu.VMEM((rows, columns), BF16),
            pltpu.VMEM((rows, columns), BF16),
            pltpu.VMEM((4, TILE, TILE), BF16),
            pltpu.VMEM((units, TILE, TILE), BF16),
            pltpu.VMEM((n, 16, TILE), F32),
            pltpu.VMEM((n, 16, TILE), F32),
            pltpu.VMEM(chunk, F32),
            pltpu.VMEM(chunk, F32),
            pltpu.VMEM(chunk, F32),
            pltpu.VMEM((8, 128), F32),
            pltpu.VMEM((m, 8, 128), F32),
            pltpu.SemaphoreType.DMA((n,)),
            pltpu.SemaphoreType.DMA((n,)),
            pltpu.SemaphoreType.DMA((n,)),
            pltpu.SemaphoreType.DMA((n,)),
            pltpu.SemaphoreType.DMA((n,)),
            pltpu.SemaphoreType.DMA((n,)),
            pltpu.SemaphoreType.DMA((m,)),
            pltpu.SemaphoreType.DMA((m,)),
            pltpu.SemaphoreType.DMA((2,)),
        ],
        compiler_params=pltpu.CompilerParams(
            collective_id=0, has_side_effects=True, vmem_limit_bytes=48 * 2**20
        ),
        name="outer_step",
    )(
        pseudo_grad[0],
        error_buf[0],
        momentum,
        sel_blocks,
        coef_index.reshape(units, TILE),
        owner_map.reshape(1, n_blocks),
        jnp.asarray(cosine_parts()),
    )
    new_params = (params.astype(F32) - update.astype(F32) * step[0, 0]).astype(BF16)
    return (new_params, new_error[None], new_momentum)


def solution(mesh):
    in_specs = (
        P("island", "fsdp", None),
        P("island", "fsdp", None),
        P("fsdp", None),
        P("island", "fsdp"),
        P("island", "fsdp"),
        P("fsdp", None),
        P("fsdp"),
    )
    out_specs = (P("fsdp", None), P("island", "fsdp", None), P("island", "fsdp"))
    return jax.shard_map(
        on_device, mesh=mesh, in_specs=in_specs, out_specs=out_specs, check_vma=False
    )
```

```python
import functools

import numpy as np

import jax
import jax.numpy as jnp
from jax import lax
from jax.experimental import pallas as pl
from jax.experimental.pallas import tpu as pltpu
from jax.sharding import PartitionSpec as P

BETA_FACTOR = 0.9
OUTER_RATE = 0.5
EPSILON = 1e-06
precise_mode = lax.Precision.HIGHEST


def cosine_table():
    freqs = jnp.arange(64, dtype=jnp.float32)[:, None]
    points = jnp.arange(64, dtype=jnp.float32)[None, :]
    scaling = jnp.where(freqs == 0.0, jnp.sqrt(1.0 / 64.0), jnp.sqrt(2.0 / 64.0))
    return scaling * jnp.cos(jnp.pi * (2.0 * points + 1.0) * freqs / 128.0)


def to_blocks(field):
    row_blocks = field.shape[0] // 64
    col_blocks = field.shape[1] // 64
    return (
        field.reshape(row_blocks, 64, col_blocks, 64)
        .transpose(0, 2, 1, 3)
        .reshape(row_blocks * col_blocks, 64, 64)
    )


def from_blocks(blocks, row_total, col_total):
    row_blocks = row_total // 64
    col_blocks = col_total // 64
    return (
        blocks.reshape(row_blocks, col_blocks, 64, 64)
        .transpose(0, 2, 1, 3)
        .reshape(row_total, col_total)
    )


def forward_blocks(cosine, blocks):
    return jnp.einsum("ij,bjk,lk->bil", cosine, blocks, cosine, precision=precise_mode)


def inverse_blocks(cosine, blocks):
    return jnp.einsum("ji,bjk,kl->bil", cosine, blocks, cosine, precision=precise_mode)


def scatter_coefs(values, positions):
    amount = values.shape[0]
    return (
        jnp.zeros((amount, 4096), jnp.float32)
        .at[jnp.arange(amount)[:, None], positions]
        .set(values)
    )


def plain_on_device(pseudo_grad, error_buf, params, momentum, sel_blocks, coef_index, owner_map):
    cosine = cosine_table()
    islands = lax.axis_size("island")
    my_island = lax.axis_index("island")
    shard_rows = params.shape[0]
    columns = params.shape[1]
    n_blocks = coef_index.shape[0]
    coef_total = coef_index.shape[1]
    capacity = momentum.shape[1] // coef_total
    summed = pseudo_grad[0].astype(jnp.float32) + error_buf[0].astype(jnp.float32)
    blocks = to_blocks(summed)
    spectra = forward_blocks(cosine, blocks).reshape(n_blocks, 4096)
    picked = jnp.take_along_axis(spectra, coef_index, axis=1)
    chosen = sel_blocks[0]
    block_ids = jnp.arange(n_blocks, dtype=jnp.int32)
    chosen_mask = jnp.any(chosen[:, None] == block_ids[None, :], axis=0).astype(jnp.float32)
    outgoing = picked * chosen_mask[:, None]
    rebuilt = inverse_blocks(cosine, scatter_coefs(outgoing, coef_index).reshape(n_blocks, 64, 64))
    new_error = from_blocks(blocks - rebuilt, shard_rows, columns).astype(jnp.bfloat16)[None]
    earlier = (owner_map[None, :] == owner_map[:, None]) & (block_ids[None, :] < block_ids[:, None])
    slot_of = jnp.sum(earlier.astype(jnp.int32), axis=1)
    target = owner_map * capacity + slot_of
    own_slots = my_island * capacity + jnp.arange(capacity, dtype=jnp.int32)
    owned_mask = target[None, :] == own_slots[:, None]
    owned_ids = jnp.sum(jnp.where(owned_mask, block_ids[None, :], 0), axis=1)
    owned_live = jnp.any(owned_mask, axis=1)
    owned_pattern = jnp.sum(jnp.where(owned_mask[:, :, None], coef_index[None, :, :], 0), axis=1)
    listed = outgoing[chosen]
    piece_values = lax.all_gather(listed, "island", axis=0, tiled=True)
    piece_ids = lax.all_gather(chosen, "island", axis=0, tiled=True)
    matches = ((piece_ids[None, :] == owned_ids[:, None]) & owned_live[:, None]).astype(jnp.float32)
    totals = jnp.dot(matches, piece_values, precision=precise_mode)
    counts = jnp.sum(matches, axis=1)
    average = totals / jnp.maximum(counts, 1.0)[:, None]
    previous = momentum[0].reshape(capacity, coef_total)
    refreshed = BETA_FACTOR * previous + average
    update_coef = average + BETA_FACTOR * refreshed
    new_momentum = refreshed.reshape(1, capacity * coef_total)
    owner_dense = inverse_blocks(
        cosine, scatter_coefs(update_coef, owned_pattern).reshape(capacity, 64, 64)
    )
    owner_dense = owner_dense.reshape(capacity, 4096).astype(jnp.bfloat16)
    gathered_dense = lax.all_gather(owner_dense, "island", axis=0, tiled=True)
    selector = (target[:, None] == jnp.arange(islands * capacity, dtype=jnp.int32)[None, :]).astype(
        jnp.bfloat16
    )
    received = jnp.dot(selector, gathered_dense, preferred_element_type=jnp.float32)
    local_square = jnp.sum(received * received)
    total_square = lax.psum(local_square, "fsdp")
    scale_root = jnp.sqrt(total_square / (shard_rows * lax.axis_size("fsdp") * columns) + EPSILON)
    shifted = from_blocks(received.reshape(n_blocks, 64, 64), shard_rows, columns)
    new_params = (params.astype(jnp.float32) - OUTER_RATE * shifted / scale_root).astype(
        jnp.bfloat16
    )
    return (new_params, new_error, new_momentum)


MESH = pl.DeviceIdType.MESH
TILE = 256
F32 = jnp.float32
BF16 = jnp.bfloat16


def cosine_parts():
    freqs = np.arange(64)[:, None]
    points = np.arange(64)[None, :]
    scaling = np.where(freqs == 0, np.sqrt(1.0 / 64.0), np.sqrt(2.0 / 64.0))
    cosine = scaling * np.cos(np.pi * (2.0 * points + 1.0) * freqs / 128.0)
    cosine = cosine.astype(np.float32)
    parts = []
    for table in (np.tile(cosine, (1, 4)), np.tile(cosine.T, (1, 4))):
        high = table.astype(BF16)
        parts += [high, (table - high.astype(np.float32)).astype(BF16)]
    return np.stack(parts)


def iota(shape, dim):
    return lax.broadcasted_iota(jnp.int32, shape, dim)


def split(value):
    high = value.astype(BF16)
    return high, (value - high.astype(F32)).astype(BF16)


def dot(a, b):
    return jnp.dot(a, b, preferred_element_type=F32)


def exact_dot(a, b, dims):
    return lax.dot_general(
        a, b, (dims, ((), ())), precision=precise_mode, preferred_element_type=F32
    )


def times_table(parts, table_ref, which):
    rows = parts[0].shape[0]
    both = dot(jnp.concatenate(parts, axis=0), table_ref[which])
    return both[:rows] + both[rows:] + dot(parts[0], table_ref[which + 1])


def table_times(table_ref, which, parts):
    stacked = table_ref[which : which + 2].reshape(2 * TILE, TILE)
    both = dot(stacked, parts[0])
    return both[:TILE] + both[TILE:] + dot(table_ref[which], parts[1])


def row_mask_of(positions):
    return iota((64, TILE), 0) == lax.shift_right_logical(positions, 6)


def col_mask_of(positions):
    cols = (positions & 63) + (iota((1, TILE), 1) & -64)
    rows = iota((TILE, TILE), 0).astype(F32).astype(BF16)
    here = rows == cols.astype(F32).astype(BF16)
    return jnp.where(here, jnp.ones((), BF16), jnp.zeros((), BF16))


def gather_unit(spectrum, positions, col_mask):
    both = dot(jnp.concatenate(split(spectrum), axis=0), col_mask)
    return jnp.sum(
        jnp.where(row_mask_of(positions), both[:64] + both[64:], 0.0), axis=0, keepdims=True
    )


def scatter_unit(parts, col_mask):
    return lax.dot_general(
        jnp.concatenate(parts, axis=0),
        col_mask,
        (((1,), (1,)), ((), ())),
        preferred_element_type=F32,
    ).astype(BF16)


def decode_tile(values, positions, masks_ref, first, half, table_ref):
    highs, lows = [], []
    for strip in range(4):
        unit = 2 * strip + half
        placed = jnp.where(row_mask_of(positions[unit : unit + 1]), values[unit : unit + 1], 0.0)
        both = scatter_unit(split(placed), masks_ref[first + unit])
        highs.append(both[:64])
        lows.append(both[64:])
    parts = (jnp.concatenate(highs, axis=0), jnp.concatenate(lows, axis=0))
    return table_times(table_ref, 2, split(times_table(parts, table_ref, 0)))


def decode_tile_short(values, positions, masks_ref, first, half, table_ref):
    pieces = []
    for strip in range(4):
        unit = 2 * strip + half
        placed = jnp.where(row_mask_of(positions[unit : unit + 1]), values[unit : unit + 1], 0.0)
        pieces.append(scatter_unit([placed.astype(BF16)], masks_ref[first + unit]))
    middle = dot(jnp.concatenate(pieces, axis=0), table_ref[0]).astype(BF16)
    return dot(table_ref[2], middle)


def column_of(row):
    extent = row.shape[1]
    diagonal = iota((extent, extent), 0) == iota((extent, extent), 1)
    column = jnp.sum(jnp.where(diagonal, row.astype(F32), 0.0), axis=1, keepdims=True)
    return column.astype(jnp.int32)


def kernel(
    n,
    m,
    elements,
    grad_hbm,
    err_hbm,
    mom_ref,
    sel_ref,
    index_ref,
    owner_ref,
    cosine_ref,
    update,
    new_err_ref,
    new_mom_ref,
    step_ref,
    grad_ref,
    err_ref,
    table_ref,
    masks,
    early,
    early_in,
    sent,
    sent_in,
    coefs,
    squares,
    squares_in,
    early_send,
    early_recv,
    sent_send,
    sent_recv,
    coefs_send,
    coefs_recv,
    squares_send,
    squares_recv,
    load_sem,
):
    me = lax.axis_index("island")
    shard = lax.axis_index("fsdp")
    units, width = index_ref.shape
    kept = 64
    slots = mom_ref.shape[1] // kept
    pairs = slots // 2
    n_blocks = owner_ref.shape[1]
    load_grad = pltpu.make_async_copy(grad_hbm, grad_ref, load_sem.at[0])
    load_err = pltpu.make_async_copy(err_hbm, err_ref, load_sem.at[1])
    load_grad.start()
    load_err.start()

    def island_peer(d):
        return lax.rem(me + d, n)

    def island_source(d):
        return lax.rem(me - d + n, n)

    barrier = pltpu.get_barrier_semaphore()
    for d in range(1, n):
        pl.semaphore_signal(barrier, inc=1, device_id=(island_peer(d), shard), device_id_type=MESH)
    for d in range(1, m):
        pl.semaphore_signal(
            barrier, inc=1, device_id=(me, lax.rem(shard + d, m)), device_id_type=MESH
        )

    lane_block = lax.shift_right_logical(iota((1, width), 1), 6)
    for q in range(4):
        keep = jnp.where(lane_block == q, 1.0, 0.0).astype(BF16)
        for which in range(4):
            table_ref[which, q * 64 : q * 64 + 64] = cosine_ref[which] * keep

    sel_row = sel_ref[...]
    sel_col = column_of(sel_row)
    in_unit = iota((units, sel_row.shape[1]), 0) == lax.shift_right_logical(sel_row, 2)
    in_lane = (sel_col & 3) == lane_block
    mask = dot(
        jnp.where(in_unit, 1.0, 0.0).astype(BF16), jnp.where(in_lane, 1.0, 0.0).astype(BF16)
    )
    owner_row = owner_ref[...]
    earlier = (column_of(owner_row) == owner_row) & (
        iota((n_blocks, n_blocks), 0) < iota((n_blocks, n_blocks), 1)
    )
    slot_row = jnp.sum(jnp.where(earlier, 1, 0), axis=0, keepdims=True)
    place = iota((slots, n_blocks), 0)
    slot_at = jnp.where(place < pairs, 2 * place, 2 * (place - pairs) + 1)
    held = jnp.where((slot_at == slot_row) & (owner_row == me), 1.0, 0.0)
    paired = jnp.concatenate([mom_ref[0:1, p * 128 : p * 128 + 128] for p in range(pairs)], axis=0)
    momentum = jnp.concatenate([paired[:, :kept], paired[:, kept:]], axis=0)
    unit_of = jnp.where(
        iota((units, n_blocks), 0) == lax.shift_right_logical(iota((units, n_blocks), 1), 2),
        1.0,
        0.0,
    )
    in_place = (iota((n_blocks, width), 0) & 3) == lane_block
    by_block = exact_dot(held, jnp.concatenate([momentum] * 4, axis=1), ((0,), (0,)))
    previous = exact_dot(unit_of, jnp.where(in_place, by_block, 0.0), ((1,), (0,)))
    for q in range(n):
        early[q, 0:8] = mask[8 * q : 8 * q + 8]
        early[q, 8:16] = previous[8 * q : 8 * q + 8]

    pl.semaphore_wait(barrier, n + m - 2)

    def early_copy(d):
        return pltpu.make_async_remote_copy(
            src_ref=early.at[island_peer(d)],
            dst_ref=early_in.at[d],
            send_sem=early_send.at[d],
            recv_sem=early_recv.at[d],
            device_id=(island_peer(d), shard),
            device_id_type=MESH,
        )

    def sent_copy(d):
        return pltpu.make_async_remote_copy(
            src_ref=sent.at[island_peer(d)],
            dst_ref=sent_in.at[d],
            send_sem=sent_send.at[d],
            recv_sem=sent_recv.at[d],
            device_id=(island_peer(d), shard),
            device_id_type=MESH,
        )

    def coefs_copy(d, slot):
        return pltpu.make_async_remote_copy(
            src_ref=coefs.at[slot],
            dst_ref=coefs.at[slot],
            send_sem=coefs_send.at[d],
            recv_sem=coefs_recv.at[d],
            device_id=(island_peer(d), shard),
            device_id_type=MESH,
        )

    def squares_copy(d):
        return pltpu.make_async_remote_copy(
            src_ref=squares,
            dst_ref=squares_in.at[d],
            send_sem=squares_send.at[d],
            recv_sem=squares_recv.at[d],
            device_id=(me, lax.rem(shard + d, m)),
            device_id_type=MESH,
        )

    def rows_of(group):
        return pl.ds(pl.multiple_of(group * TILE, TILE), TILE)

    def units_of(group):
        return pl.ds(pl.multiple_of(group * 8, 8), 8)

    def summed(group, half):
        cols = pl.ds(half * TILE, TILE)
        return grad_ref[rows_of(group), cols].astype(F32) + err_ref[rows_of(group), cols].astype(F32)

    @pl.loop(1, n)
    def _(d):
        early_copy(d).start()

    load_grad.wait()
    load_err.wait()

    def pick_group(group):
        positions = index_ref[units_of(group), :]
        picked = [None] * 8
        for half in range(2):
            middle = times_table(split(summed(group, half)), table_ref, 2)
            spectrum = table_times(table_ref, 0, split(middle))
            for strip in range(4):
                unit = 2 * strip + half
                col_mask = col_mask_of(positions[unit : unit + 1])
                masks[group * 8 + unit] = col_mask
                picked[unit] = gather_unit(
                    spectrum[strip * 64 : strip * 64 + 64], positions[unit : unit + 1], col_mask
                )
        sent[group] = jnp.concatenate(picked, axis=0) * early[group, 0:8]

    @pl.loop(1, n)
    def _(d):
        pick_group(island_peer(d))
        sent_copy(d).start()

    pick_group(me)

    def error_group(group):
        positions = index_ref[units_of(group), :]
        values = sent[group]
        for half in range(2):
            rebuilt = decode_tile_short(values, positions, masks, group * 8, half, table_ref)
            new_err_ref[rows_of(group), pl.ds(half * TILE, TILE)] = (
                summed(group, half) - rebuilt
            ).astype(BF16)

    @pl.loop(0, 3 * n // 8)
    def _(group):
        error_group(group)

    @pl.loop(1, n)
    def _(d):
        early_copy(d).wait_recv()
        sent_copy(d).wait_recv()

    totals = sent[me]
    counts = early[me, 0:8]
    owned = early[me, 8:16]
    for d in range(1, n):
        totals += sent_in[d]
        counts += early_in[d, 0:8]
        owned += early_in[d, 8:16]
    average = totals / jnp.maximum(counts, 1.0)
    coefs[me] = average + BETA_FACTOR * (BETA_FACTOR * owned + average)

    @pl.loop(1, n)
    def _(d):
        coefs_copy(d, me).start()

    @pl.loop(3 * n // 8, 3 * n // 4)
    def _(group):
        error_group(group)

    def update_group(group, total):
        positions = index_ref[units_of(group), :]
        values = coefs[group]
        for half in range(2):
            piece = decode_tile(values, positions, masks, group * 8, half, table_ref).astype(BF16)
            update[rows_of(group), pl.ds(half * TILE, TILE)] = piece
            wide = piece.astype(F32)
            total += jnp.sum((wide * wide).reshape(TILE // 8, 8, TILE), axis=0)
        return total

    total = update_group(me, jnp.zeros((8, TILE), F32))

    def arrived(d, total):
        source = island_source(d)
        coefs_copy(d, source).wait_recv()
        return update_group(source, total)

    total = lax.fori_loop(1, n, arrived, total)
    squares[...] = jnp.broadcast_to(jnp.sum(total, keepdims=True), squares.shape)
    for d in range(1, m):
        squares_copy(d).start()

    everything = jnp.concatenate([coefs[q] for q in range(n)], axis=0)
    by_block = exact_dot(unit_of, everything, ((0,), (0,)))
    wide_own = exact_dot(held, jnp.where(in_place, by_block, 0.0), ((1,), (0,)))
    own = wide_own[:, :kept]
    for j in range(1, 4):
        own += wide_own[:, j * kept : (j + 1) * kept]
    live = jnp.sum(held, axis=1, keepdims=True)
    own_average = (own - (BETA_FACTOR * BETA_FACTOR) * momentum * live) / (1.0 + BETA_FACTOR)
    refreshed = BETA_FACTOR * momentum + own_average
    refreshed = jnp.concatenate([refreshed[:pairs], refreshed[pairs:]], axis=1)
    for p in range(pairs):
        new_mom_ref[0:1, p * 128 : p * 128 + 128] = refreshed[p : p + 1]

    @pl.loop(3 * n // 4, n)
    def _(group):
        error_group(group)

    for d in range(1, m):
        squares_copy(d).wait_recv()
    total_square = squares[...]
    for d in range(1, m):
        total_square += squares_in[d]
    step = OUTER_RATE / jnp.sqrt(total_square / elements + EPSILON)
    step_ref[...] = step[0:1, 0:1]

    @pl.loop(1, n)
    def _(d):
        early_copy(d).wait_send()
        sent_copy(d).wait_send()
        coefs_copy(d, me).wait_send()

    for d in range(1, m):
        squares_copy(d).wait_send()


def on_device(pseudo_grad, error_buf, params, momentum, sel_blocks, coef_index, owner_map):
    n = lax.axis_size("island")
    m = lax.axis_size("fsdp")
    rows, columns = params.shape
    n_blocks, kept = coef_index.shape
    units = n_blocks // 4
    if rows != n * TILE or columns != 2 * TILE or kept != 64 or momentum.shape[1] % 128:
        return plain_on_device(
            pseudo_grad, error_buf, params, momentum, sel_blocks, coef_index, owner_map
        )
    slots = momentum.shape[1] // kept
    chunk = (n, 8, TILE)
    vmem = pl.BlockSpec(memory_space=pltpu.VMEM)
    update, new_error, new_momentum, step = pl.pallas_call(
        functools.partial(kernel, n, m, rows * m * columns),
        out_shape=(
            jax.ShapeDtypeStruct((rows, columns), BF16),
            jax.ShapeDtypeStruct((rows, columns), BF16),
            jax.ShapeDtypeStruct((1, slots * kept), F32),
            jax.ShapeDtypeStruct((1, 1), F32),
        ),
        in_specs=[pl.BlockSpec(memory_space=pl.ANY)] * 2 + [vmem] * 5,
        out_specs=(vmem,) * 4,
        scratch_shapes=[
            pltpu.VMEM((rows, columns), BF16),
            pltpu.VMEM((rows, columns), BF16),
            pltpu.VMEM((4, TILE, TILE), BF16),
            pltpu.VMEM((units, TILE, TILE), BF16),
            pltpu.VMEM((n, 16, TILE), F32),
            pltpu.VMEM((n, 16, TILE), F32),
            pltpu.VMEM(chunk, F32),
            pltpu.VMEM(chunk, F32),
            pltpu.VMEM(chunk, F32),
            pltpu.VMEM((8, 128), F32),
            pltpu.VMEM((m, 8, 128), F32),
            pltpu.SemaphoreType.DMA((n,)),
            pltpu.SemaphoreType.DMA((n,)),
            pltpu.SemaphoreType.DMA((n,)),
            pltpu.SemaphoreType.DMA((n,)),
            pltpu.SemaphoreType.DMA((n,)),
            pltpu.SemaphoreType.DMA((n,)),
            pltpu.SemaphoreType.DMA((m,)),
            pltpu.SemaphoreType.DMA((m,)),
            pltpu.SemaphoreType.DMA((2,)),
        ],
        compiler_params=pltpu.CompilerParams(
            collective_id=0, has_side_effects=True, vmem_limit_bytes=48 * 2**20
        ),
        name="outer_step",
    )(
        pseudo_grad[0],
        error_buf[0],
        momentum,
        sel_blocks,
        coef_index.reshape(units, TILE),
        owner_map.reshape(1, n_blocks),
        jnp.asarray(cosine_parts()),
    )
    new_params = (params.astype(F32) - update.astype(F32) * step).astype(BF16)
    return (new_params, new_error[None], new_momentum)


def solution(mesh):
    in_specs = (
        P("island", "fsdp", None),
        P("island", "fsdp", None),
        P("fsdp", None),
        P("island", "fsdp"),
        P("island", "fsdp"),
        P("fsdp", None),
        P("fsdp"),
    )
    out_specs = (P("fsdp", None), P("island", "fsdp", None), P("island", "fsdp"))
    return jax.shard_map(
        on_device, mesh=mesh, in_specs=in_specs, out_specs=out_specs, check_vma=False
    )
```
